32 devices in a mesh: ha: 4 (over y, x), wa: 8 (over z, core).
Axes of the slice: x: 2, y: 2, z: 4, core: 2. Of those that a mesh axis runs over, the one named last changes fastest.
Arguments:
- features: bfloat16 [4, 128, 256, 192], P(None, 'ha', 'wa'), may hold values from -6 to 6
- conv_first: bfloat16 [3, 3, 3, 192, 192], replicated, may hold values from -0.078125 to 0.078125
- bias_first: float32 [192], replicated, may hold values from -3 to 3
- gain_first: float32 [192], replicated, may hold values from 0.5 to 2
- conv_second: bfloat16 [3, 3, 3, 192, 192], replicated, may hold values from -0.078125 to 0.078125
- gain_second: float32 [192], replicated, may hold values from 0.5 to 2
- up_weight: bfloat16 [3, 3, 192, 96], replicated, may hold values from -0.15625 to 0.15625
- cotangent: bfloat16 [4, 256, 512, 96], P(None, 'ha', 'wa'), may hold values from -6 to 6
Outputs:
- feature_grad: bfloat16 [4, 128, 256, 192], P(None, 'ha', 'wa')
The draws below stay inside these ranges and needn't reach their ends.
All inputs are finite; a program needn't handle non-finite values.
Results may differ from the reference program's by a relative error of at most 0.0051.
Values may be sent and summed in bfloat16 or wider, within the bound.
A program may use at most 192 MiB of HBM per device.

```python
import math
import jax
import jax.numpy as jnp
from jax import lax

C = 192
C2 = 96
F = 4
H = 128
W = 256


def block_levels(rng, shape, shards, smallest, high):
    loudness = 1.0
    for dim, shards_of in shards:
        draws = jax.random.uniform(jax.random.fold_in(jax.random.fold_in(rng, 6), dim), (shards_of,), jnp.float32, smallest / len(shards), high / len(shards))
        loudness = loudness * jnp.repeat(jnp.exp(draws), shape[dim] // shards_of).reshape((-1,) + (1,) * (len(shape) - 1 - dim))
    return loudness


def noise(stream_key, dims, scale, reach, cuts=(), held_as=jnp.bfloat16):
    drawn = scale * jax.random.normal(stream_key, dims, jnp.float32)
    if cuts:
        drawn = drawn * block_levels(stream_key, dims, cuts, -0.22, 0.18)
    return jnp.clip(drawn, -reach, reach).astype(held_as)


def setup_inputs(seed: int = 0) -> dict:
    streams_of = jax.random.split(jax.random.key(seed), 9)
    features = noise(streams_of[0], (F, H, W, C), 1.0, 6.0, ((1, 4), (2, 8)))
    conv_first = noise(streams_of[1], (3, 3, 3, C, C), (27 * C) ** -0.5, 0.078125)
    bias_first = noise(streams_of[2], (C,), 0.5, 3.0, (), jnp.float32)
    gain_first = jnp.clip(jnp.exp(jax.random.uniform(streams_of[3], (C,), jnp.float32, math.log(0.5), math.log(2.0))), 0.5, 2.0)
    conv_second = noise(streams_of[4], (3, 3, 3, C, C), (27 * C) ** -0.5, 0.078125)
    gain_second = jnp.clip(jnp.exp(jax.random.uniform(streams_of[5], (C,), jnp.float32, math.log(0.5), math.log(2.0))), 0.5, 2.0)
    up_weight = noise(streams_of[6], (3, 3, C, C2), (9 * C) ** -0.5, 0.15625)
    cotangent = noise(streams_of[7], (F, 2 * H, 2 * W, C2), 1.0, 6.0, ((1, 4), (2, 8)))
    return {"features": features, "conv_first": conv_first, "bias_first": bias_first, "gain_first": gain_first, "conv_second": conv_second, "gain_second": gain_second, "up_weight": up_weight, "cotangent": cotangent}


def rms_scale(value):
    return lax.rsqrt(lax.optimization_barrier(jnp.mean(value * value, axis=-1, keepdims=True)) + 1e-06)

def silu_slope(value):
    sig = jax.nn.sigmoid(value)
    return sig * (1.0 + value * (1.0 - sig))

def rms_back(value, gain, grad):
    scale = rms_scale(value)
    scaled = gain * grad
    return scale * scaled - value * scale ** 3 * lax.optimization_barrier(jnp.mean(value * scaled, axis=-1, keepdims=True))

def causal_conv(field, weight, time_pads):
    return lax.conv_general_dilated(field[None].astype(jnp.float32), weight.astype(jnp.float32), (1, 1, 1), [time_pads, (1, 1), (1, 1)], dimension_numbers=('NDHWC', 'DHWIO', 'NDHWC'), precision=lax.Precision.HIGHEST)[0]

def reference(features, conv_first, bias_first, gain_first, conv_second, gain_second, up_weight, cotangent):
    frames, height, width, chans = features.shape
    feat_float = features.astype(jnp.float32)
    normed_first = feat_float * rms_scale(feat_float) * gain_first
    active_first = jax.nn.silu(normed_first).astype(jnp.bfloat16)
    pre_second = causal_conv(active_first, conv_first, (2, 0)) + bias_first
    normed_second = pre_second * rms_scale(pre_second) * gain_second
    up_flip = jnp.flip(up_weight, (0, 1)).swapaxes(2, 3)
    fine_grad = lax.conv_general_dilated(cotangent.astype(jnp.float32), up_flip.astype(jnp.float32), (1, 1), [(1, 1), (1, 1)], dimension_numbers=('NHWC', 'HWIO', 'NHWC'), precision=lax.Precision.HIGHEST)
    block_grad = fine_grad.reshape(frames, height, 2, width, 2, chans).sum(axis=(2, 4))
    block_low = block_grad.astype(jnp.bfloat16)
    second_flip = jnp.flip(conv_second, (0, 1, 2)).swapaxes(3, 4)
    second_grad = causal_conv(block_low, second_flip, (0, 2)) * silu_slope(normed_second)
    pre_grad = rms_back(pre_second, gain_second, second_grad).astype(jnp.bfloat16)
    first_flip = jnp.flip(conv_first, (0, 1, 2)).swapaxes(3, 4)
    first_grad = causal_conv(pre_grad, first_flip, (0, 2)) * silu_slope(normed_first)
    return (block_grad + rms_back(feat_float, gain_first, first_grad)).astype(jnp.bfloat16)
```

```python
import functools

import jax
import jax.numpy as jnp
from jax import lax
from jax.experimental import pallas as pl
from jax.experimental.pallas import tpu as pltpu
from jax.sharding import PartitionSpec as P

MESH = pl.DeviceIdType.MESH
F32, BF16 = jnp.float32, jnp.bfloat16
LEAD = 8
STEP = 8


def rms_scale(value):
    return lax.rsqrt(jnp.mean(value * value, axis=-1, keepdims=True) + 1e-06)


def silu_slope(value):
    sig = jax.nn.sigmoid(value)
    return sig * (1.0 + value * (1.0 - sig))


def rms_back(value, scale, gain, grad):
    scaled = gain * grad
    return scale * scaled - value * scale**3 * jnp.mean(value * scaled, axis=-1, keepdims=True)


class Field:
    def __init__(self, ref, parts, one_frame, rows, cols, pitch):
        self.ref, self.parts, self.one_frame = ref, parts, one_frame
        self.rows, self.cols, self.pitch = rows, cols, pitch

    def part(self, t, h):
        return h if self.one_frame else t * self.parts + h

    def cells(self, t, at):
        return jnp.concatenate([self.ref[self.part(t, h), at, :] for h in range(self.parts)], axis=1)

    def line(self, row):
        return pl.ds(pl.multiple_of(row * self.pitch + LEAD, 8), self.cols)

    def put(self, t, row, values):
        n = self.cols
        for h in range(self.parts):
            for r in range(values.shape[0] // n):
                self.ref[self.part(t, h), self.line(row + r + 1), :] = values[
                    r * n : (r + 1) * n, h * 128 : (h + 1) * 128
                ]

    def get(self, t, row, count):
        return jnp.concatenate([self.cells(t, self.line(row + r + 1)) for r in range(count)], axis=0)

    def column(self, col):
        return pl.ds(self.pitch + LEAD + col, self.rows, stride=self.pitch)

    def take_edges(self, t, stage):
        n = self.cols
        stage[0, t] = self.cells(t, pl.ds(self.pitch + LEAD, n)).astype(BF16)
        stage[1, t] = self.cells(t, pl.ds(self.rows * self.pitch + LEAD, n)).astype(BF16)
        stage[2, t] = self.cells(t, self.column(0)).astype(BF16)
        stage[3, t] = self.cells(t, self.column(n - 1)).astype(BF16)

    def set_edges(self, t, hal, cor, inside):
        up, down, left, right = inside
        n, low = self.cols, (self.rows + 1) * self.pitch + LEAD
        places = [
            (pl.ds(LEAD, n), hal[0, t].astype(F32) * up),
            (pl.ds(low, n), hal[1, t].astype(F32) * down),
            (self.column(-1), hal[2, t].astype(F32) * left),
            (self.column(n), hal[3, t].astype(F32) * right),
            (pl.ds(LEAD - 1, 1), cor[0, t].astype(F32)[15:16] * (up * left)),
            (pl.ds(LEAD + n, 1), cor[1, t].astype(F32)[0:1] * (up * right)),
            (pl.ds(low - 1, 1), cor[2, t].astype(F32)[15:16] * (down * left)),
            (pl.ds(low + n, 1), cor[3, t].astype(F32)[0:1] * (down * right)),
        ]
        for at, values in places:
            for h in range(self.parts):
                self.ref[self.part(t, h), at, :] = values[:, h * 128 : (h + 1) * 128]


def kernel(
    dims, feats, cot, bias_first, gain_first, gain_second, wu, w1_hbm, w2_hbm, w3_hbm, out,
    g0, g1, x0, x1, cf, pre, w1, w2, w3, stage, hal, cor, cstage, chal, ccor,
    w_sem, send, recv,
):
    count_h, count_w, frames, rows, cols, chans, fine_chans = dims
    me_h, me_w = lax.axis_index("ha"), lax.axis_index("wa")
    up, down = lax.rem(me_h + count_h - 1, count_h), lax.rem(me_h + 1, count_h)
    left, right = lax.rem(me_w + count_w - 1, count_w), lax.rem(me_w + 1, count_w)
    inside = [
        jnp.where(has, 1.0, 0.0).astype(F32)
        for has in (me_h > 0, me_h < count_h - 1, me_w > 0, me_w < count_w - 1)
    ]
    peers = [
        (up, me_w), (down, me_w), (me_h, left), (me_h, right),
        (up, left), (up, right), (down, left), (down, right),
    ]
    barrier = pltpu.get_barrier_semaphore()
    for peer in peers:
        pl.semaphore_signal(barrier, inc=1, device_id=peer, device_id_type=MESH)

    loads = [
        pltpu.make_async_copy(src, dst, w_sem.at[i])
        for i, (src, dst) in enumerate(((w1_hbm, w1), (w2_hbm, w2), (w3_hbm, w3)))
    ]
    for load in loads:
        load.start()

    def exchange(stage, hal, cor, sem, t=None):
        at = (slice(None),) if t is None else (t,)
        n = stage.shape[2]
        first, last = pl.ds(0, 16), pl.ds(n - 16, 16)
        routes = [
            (stage.at[(0, *at)], hal.at[(1, *at)]),
            (stage.at[(1, *at)], hal.at[(0, *at)]),
            (stage.at[(2, *at)], hal.at[(3, *at)]),
            (stage.at[(3, *at)], hal.at[(2, *at)]),
            (stage.at[(0, *at, first)], cor.at[(3, *at)]),
            (stage.at[(0, *at, last)], cor.at[(2, *at)]),
            (stage.at[(1, *at, first)], cor.at[(1, *at)]),
            (stage.at[(1, *at, last)], cor.at[(0, *at)]),
        ]
        copies = [
            pltpu.make_async_remote_copy(
                src_ref=src, dst_ref=dst, send_sem=send.at[sem, i], recv_sem=recv.at[sem, i],
                device_id=peer, device_id_type=MESH,
            )
            for i, ((src, dst), peer) in enumerate(zip(routes, peers))
        ]
        for copy in copies:
            copy.start()
        return copies

    def arrive(copies):
        for copy in copies:
            copy.wait()

    pitch = cols + 16
    active = Field(g0, 2, False, rows, cols, pitch)
    block = Field(g1, 2, False, rows, cols, pitch)
    fine = Field(cf, 1, True, 2 * rows, 2 * cols, 2 * cols + 16)
    span = STEP * cols
    steps = rows // STEP

    def over_rows(body):
        @pl.loop(0, steps)
        def _(c):
            body(c * STEP, pl.ds(pl.multiple_of(c * span, span), span))

    zero_lanes = jnp.zeros((2 * cols, 128 - fine_chans), F32)

    def load_fine(t):
        @pl.loop(0, 2 * rows)
        def _(y):
            cells = cot[t, pl.ds(pl.multiple_of(y * 2 * cols, 2 * cols), 2 * cols), :].astype(F32)
            fine.put(t, y, jnp.concatenate([cells, zero_lanes], axis=1))

    for t in range(frames):
        load_fine(t)
        fine.take_edges(t, cstage)
    pl.semaphore_wait(barrier, len(peers))
    cot_sent = exchange(cstage, chal, ccor, 0)

    def pad_lanes(values):
        return jnp.concatenate([values, jnp.zeros((values.shape[0], 256 - chans), F32)], axis=1)

    for t in range(frames):
        def first_norm(row, at, t=t):
            value = feats[t, at, :].astype(F32)
            normed = value * rms_scale(value) * gain_first[...]
            active.put(t, row, pad_lanes(normed * jax.nn.sigmoid(normed)))
        over_rows(first_norm)
        active.take_edges(t, stage.at[0])
    active_sent = exchange(stage.at[0], hal.at[0], cor.at[0], 1)

    arrive(cot_sent)
    for t in range(frames):
        load_fine(t)
        fine.set_edges(t, chal, ccor, inside)

        def coarse(row, at, t=t):
            def pairs(y):
                base = y * fine.pitch + LEAD
                before, even, odd, after = [
                    cf[0, pl.ds(base + d, cols, stride=2), :] for d in (-1, 0, 1, 2)
                ]
                return [before + even, even + odd, odd + after]

            taps = [[] for _ in range(9)]
            ahead = pairs(2 * row)
            for r in range(STEP):
                sums = [ahead] + [pairs(2 * (row + r) + d) for d in (1, 2, 3)]
                ahead = sums[2]
                for a in range(3):
                    for b in range(3):
                        taps[3 * a + b].append((sums[a][b] + sums[a + 1][b]).astype(BF16))
            lhs = jnp.concatenate([jnp.concatenate(tap, axis=0) for tap in taps], axis=1)
            block.put(t, row, pad_lanes(jnp.dot(lhs, wu[...], preferred_element_type=F32)))

        over_rows(coarse)
        block.take_edges(t, stage.at[1])
    block_sent = exchange(stage.at[1], hal.at[1], cor.at[1], 2)

    def widen(field, t, x):
        gap = jnp.zeros((cols, x.shape[-1] - 3 * chans), F32)

        @pl.loop(0, rows + 2)
        def _(row):
            line = field.cells(t, pl.ds(pl.multiple_of(row * pitch, 16), pitch))
            cells = [line[LEAD + d : LEAD + d + cols, :chans] for d in (-1, 0, 1)]
            x[t, pl.ds(pl.multiple_of(row * cols, cols), cols), :] = jnp.concatenate([*cells, gap], axis=1).astype(BF16)

    def conv(x, weight, sources, row):
        total = None
        for k, t in sources:
            lhs = jnp.concatenate(
                [x[t, pl.ds(pl.multiple_of((row + p) * cols, cols), span), :] for p in range(3)], axis=1
            )
            part = jnp.dot(lhs, weight[k], preferred_element_type=F32)
            total = part if total is None else total + part
        return total

    arrive(active_sent)
    loads[0].wait()
    for t in range(frames):
        active.set_edges(t, hal.at[0], cor.at[0], inside)
        widen(active, t, x0)

        def first_conv(row, at, t=t):
            sources = [(k, t - 2 + k) for k in range(3) if t - 2 + k >= 0]
            pre[t, at, :] = conv(x0, w1, sources, row) + bias_first[...]

        over_rows(first_conv)

    later = lambda t: [(j, t + j) for j in range(3) if t + j < frames]
    arrive(block_sent)
    loads[1].wait()
    pre_sent = [None] * frames
    for t in reversed(range(frames)):
        block.set_edges(t, hal.at[1], cor.at[1], inside)
        widen(block, t, x1)

        def second_conv(row, at, t=t):
            value = pre[t, at, :]
            scale = rms_scale(value)
            grad = conv(x1, w2, later(t), row) * silu_slope(value * scale * gain_second[...])
            active.put(t, row, pad_lanes(rms_back(value, scale, gain_second[...], grad)))

        over_rows(second_conv)
        active.take_edges(t, stage.at[2])
        pre_sent[t] = exchange(stage.at[2], hal.at[2], cor.at[2], 3 + t, t)

    loads[2].wait()
    for t in reversed(range(frames)):
        arrive(pre_sent[t])
        active.set_edges(t, hal.at[2], cor.at[2], inside)
        widen(active, t, x0)

        def third_conv(row, at, t=t):
            value = feats[t, at, :].astype(F32)
            scale = rms_scale(value)
            grad = conv(x0, w3, later(t), row) * silu_slope(value * scale * gain_first[...])
            through = rms_back(value, scale, gain_first[...], grad)
            out[t, at, :] = (block.get(t, row, STEP)[:, :chans] + through).astype(BF16)

        over_rows(third_conv)


def per_device(
    count_h, count_w, features, conv_first, bias_first, gain_first, conv_second, gain_second, up_weight, cotangent
):
    frames, rows, cols, chans = features.shape
    fine_chans = cotangent.shape[-1]
    wide = -(-3 * chans // 128) * 128

    def taps(weight):
        weight = weight.reshape(3, 3, 3 * chans, chans)
        weight = jnp.pad(weight, ((0, 0), (0, 0), (0, wide - 3 * chans), (0, 0)))
        return weight.reshape(3, 3 * wide, chans)

    flip = lambda w: jnp.flip(w, (0, 1, 2)).swapaxes(3, 4)
    up_flip = jnp.pad(jnp.flip(up_weight, (0, 1)).swapaxes(2, 3), ((0, 0), (0, 0), (0, 128 - fine_chans), (0, 0)))
    pitch, fine_pitch = cols + 16, 2 * cols + 16
    vmem, hbm = pl.BlockSpec(memory_space=pltpu.VMEM), pl.BlockSpec(memory_space=pl.ANY)
    dims = (count_h, count_w, frames, rows, cols, chans, fine_chans)
    field = pltpu.VMEM((2 * frames, (rows + 2) * pitch, 128), F32)
    spread = pltpu.VMEM((frames, (rows + 2) * cols, wide), BF16)
    weights = pltpu.VMEM((3, 3 * wide, chans), BF16)
    out = pl.pallas_call(
        functools.partial(kernel, dims),
        out_shape=jax.ShapeDtypeStruct((frames, rows * cols, chans), BF16),
        in_specs=[vmem] * 6 + [hbm] * 3,
        out_specs=vmem,
        scratch_shapes=[
            field, field, spread, spread,
            pltpu.VMEM((1, (2 * rows + 2) * fine_pitch, 128), F32),
            pltpu.VMEM((frames, rows * cols, chans), F32),
            weights, weights, weights,
            pltpu.VMEM((3, 4, frames, cols, 256), BF16),
            pltpu.VMEM((3, 4, frames, cols, 256), BF16),
            pltpu.VMEM((3, 4, frames, 16, 256), BF16),
            pltpu.VMEM((4, frames, 2 * cols, 128), BF16),
            pltpu.VMEM((4, frames, 2 * cols, 128), BF16),
            pltpu.VMEM((4, frames, 16, 128), BF16),
            pltpu.SemaphoreType.DMA((3,)),
            pltpu.SemaphoreType.DMA((3 + frames, 8)),
            pltpu.SemaphoreType.DMA((3 + frames, 8)),
        ],
        compiler_params=pltpu.CompilerParams(
            collective_id=0, has_side_effects=True, vmem_limit_bytes=60 * 2**20
        ),
    )(
        features.reshape(frames, rows * cols, chans),
        cotangent.reshape(frames, 4 * rows * cols, fine_chans),
        bias_first[None], gain_first[None], gain_second[None],
        up_flip.reshape(9 * 128, chans),
        taps(conv_first), taps(flip(conv_second)), taps(flip(conv_first)),
    )
    return out.reshape(frames, rows, cols, chans)


def solution(mesh):
    placed = (P(None, "ha", "wa", None), P(), P(), P(), P(), P(), P(), P(None, "ha", "wa", None))
    body = functools.partial(per_device, mesh.shape["ha"], mesh.shape["wa"])
    return jax.shard_map(body, mesh=mesh, in_specs=placed, out_specs=P(None, "ha", "wa", None), check_vma=False)
```

```python
import functools

import jax
import jax.numpy as jnp
from jax import lax
from jax.experimental import pallas as pl
from jax.experimental.pallas import tpu as pltpu
from jax.sharding import PartitionSpec as P

MESH = pl.DeviceIdType.MESH
F32, BF16 = jnp.float32, jnp.bfloat16
LEAD = 8
STEP = 16
FEW = 2


def rms_scale(value):
    return lax.rsqrt(jnp.mean(value * value, axis=-1, keepdims=True) + 1e-06)


def silu_slope(value):
    sig = jax.nn.sigmoid(value)
    return sig * (1.0 + value * (1.0 - sig))


def rms_back(value, scale, gain, grad):
    scaled = gain * grad
    return scale * scaled - value * scale**3 * jnp.mean(value * scaled, axis=-1, keepdims=True)


class Field:
    def __init__(self, ref, parts, one_frame, rows, cols):
        self.ref, self.parts, self.one_frame = ref, parts, one_frame
        self.rows, self.cols = rows, cols

    def part(self, t, h):
        return h if self.one_frame else t * self.parts + h

    def put(self, t, row, values):
        n = self.cols
        for h in range(self.parts):
            for r in range(values.shape[0] // n):
                self.ref[self.part(t, h), row + r + 1, pl.ds(LEAD, n), :] = values[
                    r * n : (r + 1) * n, h * 128 : (h + 1) * 128
                ]

    def line(self, t, row):
        return jnp.concatenate([self.ref[self.part(t, h), row, pl.ds(LEAD, self.cols), :] for h in range(self.parts)], axis=1)

    def get(self, t, row, count):
        return jnp.concatenate([self.line(t, row + r + 1) for r in range(count)], axis=0)

    def column(self, t, col):
        cells = [self.ref[self.part(t, h), pl.ds(1, self.rows), pl.ds(LEAD + col, 1), :] for h in range(self.parts)]
        return jnp.concatenate([c.reshape(self.rows, 128) for c in cells], axis=1)

    def take_edges(self, t, stage):
        stage[0, t] = self.line(t, 1).astype(BF16)
        stage[1, t] = self.line(t, self.rows).astype(BF16)
        stage[2, t] = self.column(t, 0).astype(BF16)
        stage[3, t] = self.column(t, self.cols - 1).astype(BF16)

    def set_edges(self, t, hal, cor, inside):
        up, down, left, right = inside
        n, low = self.cols, self.rows + 1
        lines = [
            (0, LEAD, hal[0, t].astype(F32) * up),
            (low, LEAD, hal[1, t].astype(F32) * down),
            (0, LEAD - 1, cor[0, t].astype(F32)[15:16] * (up * left)),
            (0, LEAD + n, cor[1, t].astype(F32)[0:1] * (up * right)),
            (low, LEAD - 1, cor[2, t].astype(F32)[15:16] * (down * left)),
            (low, LEAD + n, cor[3, t].astype(F32)[0:1] * (down * right)),
        ]
        columns = [
            (LEAD - 1, hal[2, t].astype(F32) * left),
            (LEAD + n, hal[3, t].astype(F32) * right),
        ]
        for h in range(self.parts):
            lanes = slice(h * 128, (h + 1) * 128)
            for row, at, values in lines:
                self.ref[self.part(t, h), row, pl.ds(at, values.shape[0]), :] = values[:, lanes]
            for at, values in columns:
                self.ref[self.part(t, h), pl.ds(1, self.rows), pl.ds(at, 1), :] = values[:, lanes].reshape(self.rows, 1, 128)


def kernel(
    dims, feats, cot, bias_first, gain_first, gain_second, up_weight, first_hbm, second_hbm, out,
    g0, g1, x0, x1, cf, boxes, pre, acc, wu, w1, w2, w3, raw, stage, hal, cor, cstage, chal, ccor,
    w_sem, send, recv,
):
    count_h, count_w, frames, rows, cols, chans, fine_chans = dims
    me_h, me_w = lax.axis_index("ha"), lax.axis_index("wa")
    up, down = lax.rem(me_h + count_h - 1, count_h), lax.rem(me_h + 1, count_h)
    left, right = lax.rem(me_w + count_w - 1, count_w), lax.rem(me_w + 1, count_w)
    inside = [
        jnp.where(has, 1.0, 0.0).astype(F32)
        for has in (me_h > 0, me_h < count_h - 1, me_w > 0, me_w < count_w - 1)
    ]
    peers = [
        (up, me_w), (down, me_w), (me_h, left), (me_h, right),
        (up, left), (up, right), (down, left), (down, right),
    ]
    barrier = pltpu.get_barrier_semaphore()
    for peer in peers:
        pl.semaphore_signal(barrier, inc=1, device_id=peer, device_id_type=MESH)

    load_first = pltpu.make_async_copy(first_hbm, raw, w_sem.at[0])
    load_second = pltpu.make_async_copy(second_hbm, raw, w_sem.at[1])
    load_first.start()
    wide = x0.shape[-1]

    def place(weight, adjoint):
        @pl.loop(0, 9)
        def _(i):
            base = pl.multiple_of(i * wide, 128)
            for q in range(3):
                tap = raw[26 - (3 * i + q)].T if adjoint else raw[3 * i + q]
                weight[pl.ds(base + q * 128, 128), :] = tap[:128]
                weight[pl.ds(base + 384 + q * 64, 64), :] = tap[128:]
            weight[pl.ds(base + 576, 64), :] = jnp.zeros((64, chans), BF16)

    def exchange(stage, hal, cor, sem, t=None):
        at = (slice(None),) if t is None else (t,)
        n = stage.shape[2]
        first, last = pl.ds(0, 16), pl.ds(n - 16, 16)
        routes = [
            (stage.at[(0, *at)], hal.at[(1, *at)]),
            (stage.at[(1, *at)], hal.at[(0, *at)]),
            (stage.at[(2, *at)], hal.at[(3, *at)]),
            (stage.at[(3, *at)], hal.at[(2, *at)]),
            (stage.at[(0, *at, first)], cor.at[(3, *at)]),
            (stage.at[(0, *at, last)], cor.at[(2, *at)]),
            (stage.at[(1, *at, first)], cor.at[(1, *at)]),
            (stage.at[(1, *at, last)], cor.at[(0, *at)]),
        ]
        copies = [
            pltpu.make_async_remote_copy(
                src_ref=src, dst_ref=dst, send_sem=send.at[sem, i], recv_sem=recv.at[sem, i],
                device_id=peer, device_id_type=MESH,
            )
            for i, ((src, dst), peer) in enumerate(zip(routes, peers))
        ]
        for copy in copies:
            copy.start()
        return copies

    def arrive(copies):
        for copy in copies:
            copy.wait()

    active = Field(g0, 2, False, rows, cols)
    block = Field(g1, 2, False, rows, cols)
    fine = Field(cf, 1, True, 2 * rows, 2 * cols)
    span = STEP * cols

    def over_rows(body):
        @pl.loop(0, rows // STEP)
        def _(c):
            body(c * STEP, pl.ds(pl.multiple_of(c * span, span), span))

    def over_cells(count, body):
        size = FEW * cols

        @pl.loop(0, count // FEW, unroll=2)
        def _(c):
            body(c * FEW, pl.ds(pl.multiple_of(c * size, size), size))

    zero_lanes = jnp.zeros((2 * cols, 128 - fine_chans), F32)

    def load_fine(t):
        @pl.loop(0, 2 * rows, unroll=8)
        def _(y):
            cells = cot[t, pl.ds(pl.multiple_of(y * 2 * cols, 2 * cols), 2 * cols), :].astype(F32)
            fine.put(t, y, jnp.concatenate([cells, zero_lanes], axis=1))

    for t in range(frames):
        load_fine(t)
        fine.take_edges(t, cstage)
    pl.semaphore_wait(barrier, len(peers))
    cot_sent = exchange(cstage, chal, ccor, 0)

    def pad_lanes(values):
        return jnp.concatenate([values, jnp.zeros((values.shape[0], 256 - chans), F32)], axis=1)

    for t in range(frames):
        def first_norm(row, at, t=t):
            value = feats[t, at, :].astype(F32)
            normed = value * rms_scale(value) * gain_first[...]
            active.put(t, row, pad_lanes(normed * jax.nn.sigmoid(normed)))
        over_cells(rows, first_norm)
        active.take_edges(t, stage.at[0])
    active_sent = exchange(stage.at[0], hal.at[0], cor.at[0], 1)

    load_first.wait()
    place(w1, False)
    place(w3, True)
    load_second.start()
    for i in range(9):
        wu[pl.ds(i * 128, fine_chans), :] = up_weight[8 - i].T
        wu[pl.ds(i * 128 + fine_chans, 128 - fine_chans), :] = jnp.zeros((128 - fine_chans, chans), BF16)

    arrive(cot_sent)
    for t in range(frames):
        load_fine(t)
        fine.set_edges(t, chal, ccor, inside)

        @pl.loop(0, rows, unroll=2)
        def _(row):
            def pairs(y):
                before, even, odd, after = [
                    cf[0, y, pl.ds(LEAD + d, cols, stride=2), :] for d in (-1, 0, 1, 2)
                ]
                return [before + even, even + odd, odd + after]

            sums = [pairs(2 * row + d) for d in range(4)]
            at = pl.ds(pl.multiple_of(row * cols, cols), cols)
            for a in range(3):
                for b in range(3):
                    boxes[at, pl.ds((3 * a + b) * 128, 128)] = (sums[a][b] + sums[a + 1][b]).astype(BF16)

        def coarse(row, at, t=t):
            block.put(t, row, pad_lanes(jnp.dot(boxes[at, :], wu[...], preferred_element_type=F32)))

        over_rows(coarse)
        block.take_edges(t, stage.at[1])
    block_sent = exchange(stage.at[1], hal.at[1], cor.at[1], 2)
    load_second.wait()
    place(w2, True)

    def widen(field, t, x):
        @pl.loop(0, rows + 2, unroll=2)
        def _(row):
            main, rest = [
                [field.ref[field.part(t, h), row, pl.ds(LEAD + d, cols), :] for d in (-1, 0, 1)] for h in range(2)
            ]
            both = jnp.concatenate([rest[0][:, :64], rest[1][:, :64]], axis=1)
            at = pl.ds(pl.multiple_of(row * cols, cols), cols)
            for i, cells in enumerate([*main, both, rest[2]]):
                x[t, at, pl.ds(i * 128, 128)] = cells.astype(BF16)

    def conv(x, weight, first, sources, row):
        lhs = jnp.concatenate(
            [x[t, pl.ds(pl.multiple_of((row + p) * cols, cols), span), :] for t in sources for p in range(3)], axis=1
        )
        rhs = weight[pl.ds(first * 3 * wide, len(sources) * 3 * wide), :]
        return jnp.dot(lhs, rhs, preferred_element_type=F32)

    arrive(active_sent)
    for t in range(frames):
        active.set_edges(t, hal.at[0], cor.at[0], inside)
        widen(active, t, x0)

        def first_conv(row, at, t=t):
            first = max(0, 2 - t)
            pre[t, at, :] = conv(x0, w1, first, [t - 2 + k for k in range(first, 3)], row) + bias_first[...]

        over_rows(first_conv)

    arrive(block_sent)
    pre_sent = [None] * frames
    for t in reversed(range(frames)):
        block.set_edges(t, hal.at[1], cor.at[1], inside)
        widen(block, t, x1)

        def second_conv(row, at, t=t):
            acc[at, :] = conv(x1, w2, 0, range(t, min(t + 3, frames)), row)

        def second_norm(row, at, t=t):
            value = pre[t, at, :]
            scale = rms_scale(value)
            grad = acc[at, :] * silu_slope(value * scale * gain_second[...])
            active.put(t, row, pad_lanes(rms_back(value, scale, gain_second[...], grad)))

        over_rows(second_conv)
        over_cells(rows, second_norm)
        active.take_edges(t, stage.at[2])
        pre_sent[t] = exchange(stage.at[2], hal.at[2], cor.at[2], 3 + t, t)

    for t in reversed(range(frames)):
        arrive(pre_sent[t])
        active.set_edges(t, hal.at[2], cor.at[2], inside)
        widen(active, t, x0)

        def third_conv(row, at, t=t):
            acc[at, :] = conv(x0, w3, 0, range(t, min(t + 3, frames)), row)

        def third_norm(row, at, t=t):
            value = feats[t, at, :].astype(F32)
            scale = rms_scale(value)
            grad = acc[at, :] * silu_slope(value * scale * gain_first[...])
            through = rms_back(value, scale, gain_first[...], grad)
            out[t, at, :] = (block.get(t, row, FEW)[:, :chans] + through).astype(BF16)

        over_rows(third_conv)
        over_cells(rows, third_norm)


def per_device(
    count_h, count_w, features, conv_first, bias_first, gain_first, conv_second, gain_second, up_weight, cotangent
):
    frames, rows, cols, chans = features.shape
    fine_chans = cotangent.shape[-1]
    wide = -(-3 * chans // 128) * 128

    pitch, fine_pitch = cols + 16, 2 * cols + 16
    vmem, hbm = pl.BlockSpec(memory_space=pltpu.VMEM), pl.BlockSpec(memory_space=pl.ANY)
    dims = (count_h, count_w, frames, rows, cols, chans, fine_chans)
    field = pltpu.VMEM((2 * frames, rows + 2, pitch, 128), F32)
    spread = pltpu.VMEM((frames, (rows + 2) * cols, wide), BF16)
    weights = pltpu.VMEM((9 * wide, chans), BF16)
    out = pl.pallas_call(
        functools.partial(kernel, dims),
        out_shape=jax.ShapeDtypeStruct((frames, rows * cols, chans), BF16),
        in_specs=[vmem] * 6 + [hbm] * 2,
        out_specs=vmem,
        scratch_shapes=[
            field, field, spread, spread,
            pltpu.VMEM((1, 2 * rows + 2, fine_pitch, 128), F32),
            pltpu.VMEM((rows * cols, 9 * 128), BF16),
            pltpu.VMEM((frames, rows * cols, chans), F32),
            pltpu.VMEM((rows * cols, chans), F32),
            pltpu.VMEM((9 * 128, chans), BF16),
            weights, weights, weights,
            pltpu.VMEM((27, chans, chans), BF16),
            pltpu.VMEM((3, 4, frames, cols, 256), BF16),
            pltpu.VMEM((3, 4, frames, cols, 256), BF16),
            pltpu.VMEM((3, 4, frames, 16, 256), BF16),
            pltpu.VMEM((4, frames, 2 * cols, 128), BF16),
            pltpu.VMEM((4, frames, 2 * cols, 128), BF16),
            pltpu.VMEM((4, frames, 16, 128), BF16),
            pltpu.SemaphoreType.DMA((2,)),
            pltpu.SemaphoreType.DMA((3 + frames, 8)),
            pltpu.SemaphoreType.DMA((3 + frames, 8)),
        ],
        compiler_params=pltpu.CompilerParams(
            collective_id=0, has_side_effects=True, vmem_limit_bytes=60 * 2**20
        ),
    )(
        features.reshape(frames, rows * cols, chans),
        cotangent.reshape(frames, 4 * rows * cols, fine_chans),
        bias_first[None], gain_first[None], gain_second[None],
        up_weight.reshape(9, chans, fine_chans),
        conv_first.reshape(27, chans, chans), conv_second.reshape(27, chans, chans),
    )
    return out.reshape(frames, rows, cols, chans)


def solution(mesh):
    placed = (P(None, "ha", "wa", None), P(), P(), P(), P(), P(), P(), P(None, "ha", "wa", None))
    body = functools.partial(per_device, mesh.shape["ha"], mesh.shape["wa"])
    return jax.shard_map(body, mesh=mesh, in_specs=placed, out_specs=P(None, "ha", "wa", None), check_vma=False)
```

```python
import functools

import jax
import jax.numpy as jnp
from jax import lax
from jax.experimental import pallas as pl
from jax.experimental.pallas import tpu as pltpu
from jax.sharding import PartitionSpec as P

MESH = pl.DeviceIdType.MESH
F32, BF16 = jnp.float32, jnp.bfloat16
LEAD = 8
STEP = 16
FEW = 2


def rms_scale(value):
    return lax.rsqrt(jnp.mean(value * value, axis=-1, keepdims=True) + 1e-06)


def silu_slope(value):
    sig = jax.nn.sigmoid(value)
    return sig * (1.0 + value * (1.0 - sig))


def rms_back(value, scale, gain, grad):
    scaled = gain * grad
    return scale * scaled - value * scale**3 * jnp.mean(value * scaled, axis=-1, keepdims=True)


def multiple(index, of):
    return index if isinstance(index, int) else pl.multiple_of(index, of)


class Field:
    def __init__(self, ref, parts, one_frame, rows, cols):
        self.ref, self.parts, self.one_frame = ref, parts, one_frame
        self.rows, self.cols = rows, cols

    def part(self, t, h):
        return h if self.one_frame else t * self.parts + h

    def put(self, t, row, values):
        n = self.cols
        for h in range(self.parts):
            for r in range(values.shape[0] // n):
                self.ref[self.part(t, h), row + r + 1, pl.ds(LEAD, n), :] = values[
                    r * n : (r + 1) * n, h * 128 : (h + 1) * 128
                ]

    def line(self, t, row):
        return jnp.concatenate([self.ref[self.part(t, h), row, pl.ds(LEAD, self.cols), :] for h in range(self.parts)], axis=1)

    def get(self, t, row, count):
        return jnp.concatenate([self.line(t, row + r + 1) for r in range(count)], axis=0)

    def column(self, t, col):
        cells = [self.ref[self.part(t, h), pl.ds(1, self.rows), pl.ds(LEAD + col, 1), :] for h in range(self.parts)]
        return jnp.concatenate([c.reshape(self.rows, 128) for c in cells], axis=1)

    def take_edges(self, t, stage):
        stage[0, t] = self.line(t, 1).astype(BF16)
        stage[1, t] = self.line(t, self.rows).astype(BF16)
        stage[2, t] = self.column(t, 0).astype(BF16)
        stage[3, t] = self.column(t, self.cols - 1).astype(BF16)

    def set_edges(self, t, hal, cor, inside):
        up, down, left, right = inside
        n, low = self.cols, self.rows + 1
        lines = [
            (0, LEAD, hal[0, t].astype(F32) * up),
            (low, LEAD, hal[1, t].astype(F32) * down),
            (0, LEAD - 1, cor[0, t].astype(F32)[15:16] * (up * left)),
            (0, LEAD + n, cor[1, t].astype(F32)[0:1] * (up * right)),
            (low, LEAD - 1, cor[2, t].astype(F32)[15:16] * (down * left)),
            (low, LEAD + n, cor[3, t].astype(F32)[0:1] * (down * right)),
        ]
        columns = [
            (LEAD - 1, hal[2, t].astype(F32) * left),
            (LEAD + n, hal[3, t].astype(F32) * right),
        ]
        for h in range(self.parts):
            lanes = slice(h * 128, (h + 1) * 128)
            for row, at, values in lines:
                self.ref[self.part(t, h), row, pl.ds(at, values.shape[0]), :] = values[:, lanes]
            for at, values in columns:
                self.ref[self.part(t, h), pl.ds(1, self.rows), pl.ds(at, 1), :] = values[:, lanes].reshape(self.rows, 1, 128)


def kernel(
    dims, feats, cot, bias_first, gain_first, gain_second, up_weight, first_hbm, second_hbm, out,
    g0, g1, x0, x1, x2, x3, y0, y1, y2, y3, cf, boxes, pre, acc0, acc1, wu, w1, w2, raw1, raw2, stage, hal, cor, cstage, chal, ccor,
    w_sem, send, recv,
):
    count_h, count_w, frames, rows, cols, chans, fine_chans = dims
    me_h, me_w = lax.axis_index("ha"), lax.axis_index("wa")
    up, down = lax.rem(me_h + count_h - 1, count_h), lax.rem(me_h + 1, count_h)
    left, right = lax.rem(me_w + count_w - 1, count_w), lax.rem(me_w + 1, count_w)
    inside = [
        jnp.where(has, 1.0, 0.0).astype(F32)
        for has in (me_h > 0, me_h < count_h - 1, me_w > 0, me_w < count_w - 1)
    ]
    peers = [
        (up, me_w), (down, me_w), (me_h, left), (me_h, right),
        (up, left), (up, right), (down, left), (down, right),
    ]
    barrier = pltpu.get_barrier_semaphore()
    for peer in peers:
        pl.semaphore_signal(barrier, inc=1, device_id=peer, device_id_type=MESH)

    load_first = pltpu.make_async_copy(first_hbm, raw1, w_sem.at[0])
    load_second = pltpu.make_async_copy(second_hbm, raw2, w_sem.at[1])
    load_first.start()
    load_second.start()
    xs, ys = (x0, x1, x2, x3), (y0, y1, y2, y3)
    wide = x0.shape[-1]

    def place(weight, raw, i, adjoint):
        base = multiple(i * wide, 128)
        for q in range(3):
            tap = raw[26 - (3 * i + q)].T if adjoint else raw[3 * i + q]
            weight[pl.ds(base + q * 128, 128), :] = tap[:128]
            weight[pl.ds(base + 384 + q * 64, 64), :] = tap[128:]
        weight[pl.ds(base + 576, 64), :] = jnp.zeros((64, chans), BF16)

    def exchange(stage, hal, cor, sem, t=None):
        at = (slice(None),) if t is None else (t,)
        n = stage.shape[2]
        first, last = pl.ds(0, 16), pl.ds(n - 16, 16)
        routes = [
            (stage.at[(0, *at)], hal.at[(1, *at)]),
            (stage.at[(1, *at)], hal.at[(0, *at)]),
            (stage.at[(2, *at)], hal.at[(3, *at)]),
            (stage.at[(3, *at)], hal.at[(2, *at)]),
            (stage.at[(0, *at, first)], cor.at[(3, *at)]),
            (stage.at[(0, *at, last)], cor.at[(2, *at)]),
            (stage.at[(1, *at, first)], cor.at[(1, *at)]),
            (stage.at[(1, *at, last)], cor.at[(0, *at)]),
        ]
        copies = [
            pltpu.make_async_remote_copy(
                src_ref=src, dst_ref=dst, send_sem=send.at[sem, i], recv_sem=recv.at[sem, i],
                device_id=peer, device_id_type=MESH,
            )
            for i, ((src, dst), peer) in enumerate(zip(routes, peers))
        ]
        for copy in copies:
            copy.start()
        return copies

    def arrive(copies):
        for copy in copies:
            copy.wait()

    active = Field(g0, 2, False, rows, cols)
    block = Field(g1, 2, False, rows, cols)
    fine = Field(cf, 1, True, 2 * rows, 2 * cols)
    span = STEP * cols

    def over_rows(body):
        @pl.loop(0, rows // STEP)
        def _(c):
            body(c * STEP, pl.ds(pl.multiple_of(c * span, span), span))

    def over_cells(count, body):
        size = FEW * cols

        @pl.loop(0, count // FEW, unroll=2)
        def _(c):
            body(c * FEW, pl.ds(pl.multiple_of(c * size, size), size))

    zero_lanes = jnp.zeros((2 * cols, 128 - fine_chans), F32)

    def load_fine(t):
        @pl.loop(0, 2 * rows, unroll=8)
        def _(y):
            cells = cot[t, pl.ds(pl.multiple_of(y * 2 * cols, 2 * cols), 2 * cols), :].astype(F32)
            fine.put(t, y, jnp.concatenate([cells, zero_lanes], axis=1))

    for t in range(frames):
        load_fine(t)
        fine.take_edges(t, cstage)
    pl.semaphore_wait(barrier, len(peers))
    cot_sent = exchange(cstage, chal, ccor, 0)

    def pad_lanes(values):
        return jnp.concatenate([values, jnp.zeros((values.shape[0], 256 - chans), F32)], axis=1)

    for t in range(frames):
        def first_norm(row, at, t=t):
            value = feats[t, at, :].astype(F32)
            normed = value * rms_scale(value) * gain_first[...]
            active.put(t, row, pad_lanes(normed * jax.nn.sigmoid(normed)))
        over_cells(rows, first_norm)
        active.take_edges(t, stage.at[0])
    active_sent = exchange(stage.at[0], hal.at[0], cor.at[0], 1)

    load_first.wait()

    @pl.loop(0, 9)
    def _(i):
        place(w1, raw1, i, False)

    for i in range(9):
        wu[pl.ds(i * 128, fine_chans), :] = up_weight[8 - i].T
        wu[pl.ds(i * 128 + fine_chans, 128 - fine_chans), :] = jnp.zeros((128 - fine_chans, chans), BF16)

    arrive(cot_sent)
    for t in range(frames):
        load_fine(t)
        fine.set_edges(t, chal, ccor, inside)

        @pl.loop(0, rows // 4)
        def _(c):
            def pairs(y):
                before, even, odd, after = [
                    cf[0, y, pl.ds(LEAD + d, cols, stride=2), :] for d in (-1, 0, 1, 2)
                ]
                return [before + even, even + odd, odd + after]

            sums = [pairs(8 * c + d) for d in range(10)]
            for r in range(4):
                at = pl.ds(pl.multiple_of((4 * c + r) * cols, cols), cols)
                for a in range(3):
                    for b in range(3):
                        boxes[at, pl.ds((3 * a + b) * 128, 128)] = (
                            sums[2 * r + a][b] + sums[2 * r + a + 1][b]
                        ).astype(BF16)

        def coarse(row, at, t=t):
            block.put(t, row, pad_lanes(jnp.dot(boxes[at, :], wu[...], preferred_element_type=F32)))

        over_rows(coarse)
        block.take_edges(t, stage.at[1])
    block_sent = exchange(stage.at[1], hal.at[1], cor.at[1], 2)
    load_second.wait()

    def widen(field, t, x, low, high):
        for row in range(low, high):
            main, rest = [
                [field.ref[field.part(t, h), row, pl.ds(LEAD + d, cols), :] for d in (-1, 0, 1)] for h in range(2)
            ]
            both = jnp.concatenate([rest[0][:, :64], rest[1][:, :64]], axis=1)
            for i, cells in enumerate([*main, both, rest[2]]):
                x[pl.ds(row * cols, cols), pl.ds(i * 128, 128)] = cells.astype(BF16)

    def conv(x, weight, first, sources, row):
        lhs = jnp.concatenate([x[t][pl.ds((row + p) * cols, span), :] for t in sources for p in range(3)], axis=1)
        rhs = weight[pl.ds(first * 3 * wide, len(sources) * 3 * wide), :]
        return jnp.dot(lhs, rhs, preferred_element_type=F32)

    def first_conv(t, row, acc):
        first = max(0, 2 - t)
        at = pl.ds(row * cols, span)
        pre[t, at, :] = conv(xs, w1, first, [t - 2 + k for k in range(first, 3)], row) + bias_first[...]

    def second_conv(t, row, acc):
        acc[...] = conv(ys, w2, 0, range(t, min(t + 3, frames)), row)

    def third_conv(t, row, acc):
        acc[...] = conv(xs, w1, 0, range(t, min(t + 3, frames)), row)

    def second_norm(t, row, acc):
        for r in range(0, STEP, FEW):
            value = pre[t, pl.ds((row + r) * cols, FEW * cols), :]
            scale = rms_scale(value)
            grad = acc[pl.ds(r * cols, FEW * cols), :] * silu_slope(value * scale * gain_second[...])
            active.put(t, row + r, pad_lanes(rms_back(value, scale, gain_second[...], grad)))

    def third_norm(t, row, acc):
        for r in range(0, STEP, FEW):
            at = pl.ds((row + r) * cols, FEW * cols)
            value = feats[t, at, :].astype(F32)
            scale = rms_scale(value)
            grad = acc[pl.ds(r * cols, FEW * cols), :] * silu_slope(value * scale * gain_first[...])
            through = rms_back(value, scale, gain_first[...], grad)
            out[t, at, :] = (block.get(t, row + r, FEW)[:, :chans] + through).astype(BF16)

    arrive(active_sent)
    active.set_edges(0, hal.at[0], cor.at[0], inside)
    widen(active, 0, x0, 0, rows + 2)

    halves = rows // STEP
    order = [("first", t, c) for t in range(frames) for c in range(halves)]
    order += [(stage_of, t, c) for stage_of in ("second", "third") for t in reversed(range(frames)) for c in range(halves)]
    convs = {"first": first_conv, "second": second_conv, "third": third_conv}
    norms = {"second": second_norm, "third": third_norm}
    pre_sent = [None] * frames
    before = None
    for count, (name, t, c) in enumerate(order):
        if name == "first":
            ahead = (active, t + 1, xs, 0) if t + 1 < frames else (block, frames - 1, ys, 1)
        elif name == "second":
            ahead = (block, t - 1, ys, 1) if t > 0 else (active, frames - 1, xs, 2)
        else:
            ahead = (active, t - 1, xs, 2) if t > 0 else None
        if c == 0 and ahead is not None:
            field, other, _, slot = ahead
            if name == "first" and slot == 1:
                arrive(block_sent)
            if slot == 2:
                arrive(pre_sent[other])
            field.set_edges(other, hal.at[slot], cor.at[slot], inside)
        taps_at = [i for i in range(9) if i * frames * halves // 9 == count % (frames * halves)]

        @pl.when(me_h >= 0)
        def _():
            if before is not None:
                norms[before[0]](before[1], before[2] * STEP, (acc0, acc1)[(count - 1) % 2])
            convs[name](t, c * STEP, (acc0, acc1)[count % 2])
            if ahead is not None:
                share = (rows + 2) // halves
                widen(ahead[0], ahead[1], ahead[2][ahead[1]], c * share, rows + 2 if c == halves - 1 else (c + 1) * share)
            for i in taps_at:
                if name == "first":
                    place(w2, raw2, i, True)
                if name == "second":
                    place(w1, raw1, i, True)

        if before is not None and before[0] == "second" and before[2] == halves - 1:
            done = before[1]
            active.take_edges(done, stage.at[2])
            pre_sent[done] = exchange(stage.at[2], hal.at[2], cor.at[2], 3 + done, done)
        before = (name, t, c) if name in norms else None
    norms[before[0]](before[1], before[2] * STEP, (acc0, acc1)[(len(order) - 1) % 2])


def per_device(
    count_h, count_w, features, conv_first, bias_first, gain_first, conv_second, gain_second, up_weight, cotangent
):
    frames, rows, cols, chans = features.shape
    fine_chans = cotangent.shape[-1]
    wide = -(-3 * chans // 128) * 128

    pitch, fine_pitch = cols + 16, 2 * cols + 16
    vmem, hbm = pl.BlockSpec(memory_space=pltpu.VMEM), pl.BlockSpec(memory_space=pl.ANY)
    dims = (count_h, count_w, frames, rows, cols, chans, fine_chans)
    field = pltpu.VMEM((2 * frames, rows + 2, pitch, 128), F32)
    spread = [pltpu.VMEM(((rows + 2) * cols, wide), BF16)] * (2 * frames)
    weights = pltpu.VMEM((9 * wide, chans), BF16)
    out = pl.pallas_call(
        functools.partial(kernel, dims),
        out_shape=jax.ShapeDtypeStruct((frames, rows * cols, chans), BF16),
        in_specs=[vmem] * 6 + [hbm] * 2,
        out_specs=vmem,
        scratch_shapes=[
            field, field, *spread,
            pltpu.VMEM((1, 2 * rows + 2, fine_pitch, 128), F32),
            pltpu.VMEM((rows * cols, 9 * 128), BF16),
            pltpu.VMEM((frames, rows * cols, chans), F32),
            pltpu.VMEM((STEP * cols, chans), F32),
            pltpu.VMEM((STEP * cols, chans), F32),
            pltpu.VMEM((9 * 128, chans), BF16),
            weights, weights,
            pltpu.VMEM((27, chans, chans), BF16),
            pltpu.VMEM((27, chans, chans), BF16),
            pltpu.VMEM((3, 4, frames, cols, 256), BF16),
            pltpu.VMEM((3, 4, frames, cols, 256), BF16),
            pltpu.VMEM((3, 4, frames, 16, 256), BF16),
            pltpu.VMEM((4, frames, 2 * cols, 128), BF16),
            pltpu.VMEM((4, frames, 2 * cols, 128), BF16),
            pltpu.VMEM((4, frames, 16, 128), BF16),
            pltpu.SemaphoreType.DMA((2,)),
            pltpu.SemaphoreType.DMA((3 + frames, 8)),
            pltpu.SemaphoreType.DMA((3 + frames, 8)),
        ],
        compiler_params=pltpu.CompilerParams(
            collective_id=0, has_side_effects=True, vmem_limit_bytes=60 * 2**20
        ),
    )(
        features.reshape(frames, rows * cols, chans),
        cotangent.reshape(frames, 4 * rows * cols, fine_chans),
        bias_first[None], gain_first[None], gain_second[None],
        up_weight.reshape(9, chans, fine_chans),
        conv_first.reshape(27, chans, chans), conv_second.reshape(27, chans, chans),
    )
    return out.reshape(frames, rows, cols, chans)


def solution(mesh):
    placed = (P(None, "ha", "wa", None), P(), P(), P(), P(), P(), P(), P(None, "ha", "wa", None))
    body = functools.partial(per_device, mesh.shape["ha"], mesh.shape["wa"])
    return jax.shard_map(body, mesh=mesh, in_specs=placed, out_specs=P(None, "ha", "wa", None), check_vma=False)
```

```python
import functools

import jax
import jax.numpy as jnp
from jax import lax
from jax.experimental import pallas as pl
from jax.experimental.pallas import tpu as pltpu
from jax.sharding import PartitionSpec as P

MESH = pl.DeviceIdType.MESH
F32, BF16 = jnp.float32, jnp.bfloat16
LEAD = 8
STEP = 16
FEW = 2


def rms_scale(value):
    return lax.rsqrt(jnp.mean(value * value, axis=-1, keepdims=True) + 1e-06)


def silu_slope(value):
    sig = jax.nn.sigmoid(value)
    return sig * (1.0 + value * (1.0 - sig))


def rms_back(value, scale, gain, grad):
    scaled = gain * grad
    return scale * scaled - value * scale**3 * jnp.mean(value * scaled, axis=-1, keepdims=True)


def multiple(index, of):
    return index if isinstance(index, int) else pl.multiple_of(index, of)


class Field:
    def __init__(self, ref, parts, one_frame, rows, cols):
        self.ref, self.parts, self.one_frame = ref, parts, one_frame
        self.rows, self.cols = rows, cols

    def part(self, t, h):
        return h if self.one_frame else t * self.parts + h

    def put(self, t, row, values):
        n = self.cols
        for h in range(self.parts):
            for r in range(values.shape[0] // n):
                self.ref[self.part(t, h), row + r + 1, pl.ds(LEAD, n), :] = values[
                    r * n : (r + 1) * n, h * 128 : (h + 1) * 128
                ]

    def line(self, t, row):
        return jnp.concatenate([self.ref[self.part(t, h), row, pl.ds(LEAD, self.cols), :] for h in range(self.parts)], axis=1)

    def get(self, t, row, count):
        return jnp.concatenate([self.line(t, row + r + 1) for r in range(count)], axis=0)

    def column(self, t, col):
        cells = [self.ref[self.part(t, h), pl.ds(1, self.rows), pl.ds(LEAD + col, 1), :] for h in range(self.parts)]
        return jnp.concatenate([c.reshape(self.rows, 128) for c in cells], axis=1)

    def take_edges(self, t, stage):
        stage[0, t] = self.line(t, 1).astype(BF16)
        stage[1, t] = self.line(t, self.rows).astype(BF16)
        stage[2, t] = self.column(t, 0).astype(BF16)
        stage[3, t] = self.column(t, self.cols - 1).astype(BF16)

    def set_edges(self, t, hal, cor, inside):
        up, down, left, right = inside
        n, low = self.cols, self.rows + 1
        lines = [
            (0, LEAD, hal[0, t].astype(F32) * up),
            (low, LEAD, hal[1, t].astype(F32) * down),
            (0, LEAD - 1, cor[0, t].astype(F32)[15:16] * (up * left)),
            (0, LEAD + n, cor[1, t].astype(F32)[0:1] * (up * right)),
            (low, LEAD - 1, cor[2, t].astype(F32)[15:16] * (down * left)),
            (low, LEAD + n, cor[3, t].astype(F32)[0:1] * (down * right)),
        ]
        columns = [
            (LEAD - 1, hal[2, t].astype(F32) * left),
            (LEAD + n, hal[3, t].astype(F32) * right),
        ]
        for h in range(self.parts):
            lanes = slice(h * 128, (h + 1) * 128)
            for row, at, values in lines:
                self.ref[self.part(t, h), row, pl.ds(at, values.shape[0]), :] = values[:, lanes]
            for at, values in columns:
                self.ref[self.part(t, h), pl.ds(1, self.rows), pl.ds(at, 1), :] = values[:, lanes].reshape(self.rows, 1, 128)


def kernel(
    dims, feats, cot, bias_first, gain_first, gain_second, up_weight, first_hbm, second_hbm, out,
    g0, g1, x0, x1, x2, x3, y0, y1, y2, y3, cf, boxes, pre, acc0, acc1, wu, w1, w2, raw1, raw2, stage, hal, cor, cstage, chal, ccor,
    w_sem, send, recv,
):
    count_h, count_w, frames, rows, cols, chans, fine_chans = dims
    me_h, me_w = lax.axis_index("ha"), lax.axis_index("wa")
    up, down = lax.rem(me_h + count_h - 1, count_h), lax.rem(me_h + 1, count_h)
    left, right = lax.rem(me_w + count_w - 1, count_w), lax.rem(me_w + 1, count_w)
    inside = [
        jnp.where(has, 1.0, 0.0).astype(F32)
        for has in (me_h > 0, me_h < count_h - 1, me_w > 0, me_w < count_w - 1)
    ]
    peers = [
        (up, me_w), (down, me_w), (me_h, left), (me_h, right),
        (up, left), (up, right), (down, left), (down, right),
    ]
    barrier = pltpu.get_barrier_semaphore()
    for peer in peers:
        pl.semaphore_signal(barrier, inc=1, device_id=peer, device_id_type=MESH)

    load_first = pltpu.make_async_copy(first_hbm, raw1, w_sem.at[0])
    load_second = pltpu.make_async_copy(second_hbm, raw2, w_sem.at[1])
    load_first.start()
    load_second.start()
    xs, ys = (x0, x1, x2, x3), (y0, y1, y2, y3)
    wide = x0.shape[-1]

    def place(weight, raw, i, adjoint):
        base = multiple(i * wide, 128)
        for q in range(3):
            tap = raw[26 - (3 * i + q)].T if adjoint else raw[3 * i + q]
            weight[pl.ds(base + q * 128, 128), :] = tap[:128]
            weight[pl.ds(base + 384 + q * 64, 64), :] = tap[128:]
        weight[pl.ds(base + 576, 64), :] = jnp.zeros((64, chans), BF16)

    def exchange(stage, hal, cor, sem, t=None):
        at = (slice(None),) if t is None else (t,)
        n = stage.shape[2]
        first, last = pl.ds(0, 16), pl.ds(n - 16, 16)
        routes = [
            (stage.at[(0, *at)], hal.at[(1, *at)]),
            (stage.at[(1, *at)], hal.at[(0, *at)]),
            (stage.at[(2, *at)], hal.at[(3, *at)]),
            (stage.at[(3, *at)], hal.at[(2, *at)]),
            (stage.at[(0, *at, first)], cor.at[(3, *at)]),
            (stage.at[(0, *at, last)], cor.at[(2, *at)]),
            (stage.at[(1, *at, first)], cor.at[(1, *at)]),
            (stage.at[(1, *at, last)], cor.at[(0, *at)]),
        ]
        copies = [
            pltpu.make_async_remote_copy(
                src_ref=src, dst_ref=dst, send_sem=send.at[sem, i], recv_sem=recv.at[sem, i],
                device_id=peer, device_id_type=MESH,
            )
            for i, ((src, dst), peer) in enumerate(zip(routes, peers))
        ]
        for copy in copies:
            copy.start()
        return copies

    def arrive(copies):
        for copy in copies:
            copy.wait()

    active = Field(g0, 2, False, rows, cols)
    block = Field(g1, 2, False, rows, cols)
    fine = Field(cf, 1, True, 2 * rows, 2 * cols)
    span = STEP * cols

    def over_rows(body):
        @pl.loop(0, rows // STEP)
        def _(c):
            body(c * STEP, pl.ds(pl.multiple_of(c * span, span), span))

    def over_cells(count, body):
        size = FEW * cols

        @pl.loop(0, count // FEW, unroll=4)
        def _(c):
            body(c * FEW, pl.ds(pl.multiple_of(c * size, size), size))

    zero_lanes = jnp.zeros((2 * cols, 128 - fine_chans), F32)

    def load_fine(t):
        @pl.loop(0, 2 * rows, unroll=8)
        def _(y):
            cells = cot[t, pl.ds(pl.multiple_of(y * 2 * cols, 2 * cols), 2 * cols), :].astype(F32)
            fine.put(t, y, jnp.concatenate([cells, zero_lanes], axis=1))

    def load_border(t):
        length = 2 * cols
        for y in (0, 2 * rows - 1):
            fine.put(t, y, jnp.concatenate([cot[t, pl.ds(y * length, length), :].astype(F32), zero_lanes], axis=1))

        @pl.loop(0, 2 * rows, unroll=8)
        def _(y):
            for side in (0, length - 16):
                cells = cot[t, pl.ds(pl.multiple_of(y * length, length) + side, 16), :].astype(F32)
                cf[0, y + 1, pl.ds(LEAD + side, 16), :] = jnp.concatenate([cells, zero_lanes[:16]], axis=1)

    for t in range(frames):
        load_border(t)
        fine.take_edges(t, cstage)
    pl.semaphore_wait(barrier, len(peers))
    cot_sent = exchange(cstage, chal, ccor, 0)

    def pad_lanes(values):
        return jnp.concatenate([values, jnp.zeros((values.shape[0], 256 - chans), F32)], axis=1)

    for t in range(frames):
        def first_norm(row, at, t=t):
            value = feats[t, at, :].astype(F32)
            normed = value * rms_scale(value) * gain_first[...]
            active.put(t, row, pad_lanes(normed * jax.nn.sigmoid(normed)))
        over_cells(rows, first_norm)
        active.take_edges(t, stage.at[0])
    active_sent = exchange(stage.at[0], hal.at[0], cor.at[0], 1)

    load_first.wait()

    @pl.loop(0, 9)
    def _(i):
        place(w1, raw1, i, False)

    for i in range(9):
        wu[pl.ds(i * 128, fine_chans), :] = up_weight[8 - i].T
        wu[pl.ds(i * 128 + fine_chans, 128 - fine_chans), :] = jnp.zeros((128 - fine_chans, chans), BF16)

    arrive(cot_sent)
    for t in range(frames):
        load_fine(t)
        fine.set_edges(t, chal, ccor, inside)

        @pl.loop(0, rows // 4, unroll=2)
        def _(c):
            def pairs(y):
                before, even, odd, after = [
                    cf[0, y, pl.ds(LEAD + d, cols, stride=2), :] for d in (-1, 0, 1, 2)
                ]
                return [before + even, even + odd, odd + after]

            sums = [pairs(8 * c + d) for d in range(10)]
            for r in range(4):
                at = pl.ds(pl.multiple_of((4 * c + r) * cols, cols), cols)
                for a in range(3):
                    for b in range(3):
                        boxes[at, pl.ds((3 * a + b) * 128, 128)] = (
                            sums[2 * r + a][b] + sums[2 * r + a + 1][b]
                        ).astype(BF16)

        def coarse(row, at, t=t):
            block.put(t, row, pad_lanes(jnp.dot(boxes[at, :], wu[...], preferred_element_type=F32)))

        over_rows(coarse)
        block.take_edges(t, stage.at[1])
    block_sent = exchange(stage.at[1], hal.at[1], cor.at[1], 2)
    load_second.wait()

    def widen(field, t, x, low, high):
        for row in range(low, high):
            main, rest = [
                [field.ref[field.part(t, h), row, pl.ds(LEAD + d, cols), :] for d in (-1, 0, 1)] for h in range(2)
            ]
            both = jnp.concatenate([rest[0][:, :64], rest[1][:, :64]], axis=1)
            for i, cells in enumerate([*main, both, rest[2]]):
                x[pl.ds(row * cols, cols), pl.ds(i * 128, 128)] = cells.astype(BF16)

    def conv(x, weight, first, sources, row):
        lhs = jnp.concatenate([x[t][pl.ds((row + p) * cols, span), :] for t in sources for p in range(3)], axis=1)
        rhs = weight[pl.ds(first * 3 * wide, len(sources) * 3 * wide), :]
        return jnp.dot(lhs, rhs, preferred_element_type=F32)

    def first_conv(t, row, acc):
        first = max(0, 2 - t)
        at = pl.ds(row * cols, span)
        pre[t, at, :] = conv(xs, w1, first, [t - 2 + k for k in range(first, 3)], row) + bias_first[...]

    def second_conv(t, row, acc):
        acc[...] = conv(ys, w2, 0, range(t, min(t + 3, frames)), row)

    def third_conv(t, row, acc):
        acc[...] = conv(xs, w1, 0, range(t, min(t + 3, frames)), row)

    def second_norm(t, row, acc):
        for r in range(0, STEP, FEW):
            value = pre[t, pl.ds((row + r) * cols, FEW * cols), :]
            scale = rms_scale(value)
            grad = acc[pl.ds(r * cols, FEW * cols), :] * silu_slope(value * scale * gain_second[...])
            active.put(t, row + r, pad_lanes(rms_back(value, scale, gain_second[...], grad)))

    def third_norm(t, row, acc):
        for r in range(0, STEP, FEW):
            at = pl.ds((row + r) * cols, FEW * cols)
            value = feats[t, at, :].astype(F32)
            scale = rms_scale(value)
            grad = acc[pl.ds(r * cols, FEW * cols), :] * silu_slope(value * scale * gain_first[...])
            through = rms_back(value, scale, gain_first[...], grad)
            out[t, at, :] = (block.get(t, row + r, FEW)[:, :chans] + through).astype(BF16)

    arrive(active_sent)
    active.set_edges(0, hal.at[0], cor.at[0], inside)
    widen(active, 0, x0, 0, rows + 2)

    halves = rows // STEP
    order = [("first", t, c) for t in range(frames) for c in range(halves)]
    order += [(stage_of, t, c) for stage_of in ("second", "third") for t in reversed(range(frames)) for c in range(halves)]
    convs = {"first": first_conv, "second": second_conv, "third": third_conv}
    norms = {"second": second_norm, "third": third_norm}
    pre_sent = [None] * frames
    before = None
    for count, (name, t, c) in enumerate(order):
        if name == "first":
            ahead = (active, t + 1, xs, 0) if t + 1 < frames else (block, frames - 1, ys, 1)
        elif name == "second":
            ahead = (block, t - 1, ys, 1) if t > 0 else (active, frames - 1, xs, 2)
        else:
            ahead = (active, t - 1, xs, 2) if t > 0 else None
        if c == 0 and ahead is not None:
            field, other, _, slot = ahead
            if name == "first" and slot == 1:
                arrive(block_sent)
            if slot == 2:
                arrive(pre_sent[other])
            field.set_edges(other, hal.at[slot], cor.at[slot], inside)
        taps_at = [i for i in range(9) if i * frames * halves // 9 == count % (frames * halves)]

        @pl.when(me_h >= 0)
        def _():
            if before is not None:
                norms[before[0]](before[1], before[2] * STEP, (acc0, acc1)[(count - 1) % 2])
            convs[name](t, c * STEP, (acc0, acc1)[count % 2])
            if ahead is not None:
                share = (rows + 2) // halves
                widen(ahead[0], ahead[1], ahead[2][ahead[1]], c * share, rows + 2 if c == halves - 1 else (c + 1) * share)
            for i in taps_at:
                if name == "first":
                    place(w2, raw2, i, True)
                if name == "second":
                    place(w1, raw1, i, True)

        if before is not None and before[0] == "second" and before[2] == halves - 1:
            done = before[1]
            active.take_edges(done, stage.at[2])
            pre_sent[done] = exchange(stage.at[2], hal.at[2], cor.at[2], 3 + done, done)
        before = (name, t, c) if name in norms else None
    norms[before[0]](before[1], before[2] * STEP, (acc0, acc1)[(len(order) - 1) % 2])


def per_device(
    count_h, count_w, features, conv_first, bias_first, gain_first, conv_second, gain_second, up_weight, cotangent
):
    frames, rows, cols, chans = features.shape
    fine_chans = cotangent.shape[-1]
    wide = -(-3 * chans // 128) * 128

    pitch, fine_pitch = cols + 16, 2 * cols + 16
    vmem, hbm = pl.BlockSpec(memory_space=pltpu.VMEM), pl.BlockSpec(memory_space=pl.ANY)
    dims = (count_h, count_w, frames, rows, cols, chans, fine_chans)
    field = pltpu.VMEM((2 * frames, rows + 2, pitch, 128), F32)
    spread = [pltpu.VMEM(((rows + 2) * cols, wide), BF16)] * (2 * frames)
    weights = pltpu.VMEM((9 * wide, chans), BF16)
    out = pl.pallas_call(
        functools.partial(kernel, dims),
        out_shape=jax.ShapeDtypeStruct((frames, rows * cols, chans), BF16),
        in_specs=[vmem] * 6 + [hbm] * 2,
        out_specs=vmem,
        scratch_shapes=[
            field, field, *spread,
            pltpu.VMEM((1, 2 * rows + 2, fine_pitch, 128), F32),
            pltpu.VMEM((rows * cols, 9 * 128), BF16),
            pltpu.VMEM((frames, rows * cols, chans), F32),
            pltpu.VMEM((STEP * cols, chans), F32),
            pltpu.VMEM((STEP * cols, chans), F32),
            pltpu.VMEM((9 * 128, chans), BF16),
            weights, weights,
            pltpu.VMEM((27, chans, chans), BF16),
            pltpu.VMEM((27, chans, chans), BF16),
            pltpu.VMEM((3, 4, frames, cols, 256), BF16),
            pltpu.VMEM((3, 4, frames, cols, 256), BF16),
            pltpu.VMEM((3, 4, frames, 16, 256), BF16),
            pltpu.VMEM((4, frames, 2 * cols, 128), BF16),
            pltpu.VMEM((4, frames, 2 * cols, 128), BF16),
            pltpu.VMEM((4, frames, 16, 128), BF16),
            pltpu.SemaphoreType.DMA((2,)),
            pltpu.SemaphoreType.DMA((3 + frames, 8)),
            pltpu.SemaphoreType.DMA((3 + frames, 8)),
        ],
        compiler_params=pltpu.CompilerParams(
            collective_id=0, has_side_effects=True, vmem_limit_bytes=60 * 2**20
        ),
    )(
        features.reshape(frames, rows * cols, chans),
        cotangent.reshape(frames, 4 * rows * cols, fine_chans),
        bias_first[None], gain_first[None], gain_second[None],
        up_weight.reshape(9, chans, fine_chans),
        conv_first.reshape(27, chans, chans), conv_second.reshape(27, chans, chans),
    )
    return out.reshape(frames, rows, cols, chans)


def solution(mesh):
    placed = (P(None, "ha", "wa", None), P(), P(), P(), P(), P(), P(), P(None, "ha", "wa", None))
    body = functools.partial(per_device, mesh.shape["ha"], mesh.shape["wa"])
    return jax.shard_map(body, mesh=mesh, in_specs=placed, out_specs=P(None, "ha", "wa", None), check_vma=False)
```
